256 devices in a mesh: leaf: 32 (over z_hi, y, core), blk: 8 (over z_lo, x).
Axes of the slice: x: 4, y: 4, z: 8 (z_hi: 4, z_lo: 2; z = z_hi * 2 + z_lo), core: 2. Of those that a mesh axis runs over, the one named last changes fastest.
Arguments:
- sample: float32 [3, 229376, 512], P(None, ('leaf', 'blk')), may hold values from -6 to 6
- probes: float32 [3, 229376, 512], P(None, ('leaf', 'blk')), may hold values from -0.03125 to 0.03125
- skeleton_rows: int32 [14, 128], replicated, may hold values from 0 to 114687, as said below
Outputs:
- interpolants: float32 [3, 229376, 128], P(None, ('leaf', 'blk'))
- coupling: float32 [3, 32, 128, 128], P(None, 'leaf')
The draws below stay inside these ranges and needn't reach their ends.
Inputs may be any that keep to these rules, and one draw needn't show every extreme that they name: `skeleton_rows`: list 2^(l+1) - 2 + j belongs to node j of level l; it holds 128 distinct row indices counted from the node's first row, below 229376 / 2^(l+1); its first entry is always 0 and its last entry is always the node's last row.
All inputs are finite; a program needn't handle non-finite values.
Results may differ from the reference program's by a relative error of at most 0.0003.
Values sent between devices are 32-bit elements; how exact they have to be, the bound alone decides.
A program may use at most 128 MiB of HBM per device.

```python
import jax
import jax.numpy as jnp
from jax import lax

SAMPLES = 512
SKEL = 128
LEVELS = 3
GROUPS = 32
NROWS = 229376


def draw_skeleton_rows(key, part):
    key = jax.random.fold_in(key, 7)
    listed = []
    for level_id in range(LEVELS):
        nodes = 2 ** (level_id + 1)
        node_rows = NROWS // nodes
        for node_id in range(nodes):
            sub_key = jax.random.fold_in(key, nodes - 2 + node_id)
            chosen = (jax.random.permutation(sub_key, node_rows - 2)[:SKEL - 2] + 1).astype(jnp.int32)
            listed.append(jnp.concatenate([jnp.zeros((1,), jnp.int32), chosen, jnp.full((1,), node_rows - 1, jnp.int32)]))
    return jnp.stack(listed)


def shard_levels(key, dims, pieces, least, top_value):
    def one(position, shards_of):
        steps = jax.random.uniform(jax.random.fold_in(jax.random.fold_in(key, 6), position), (shards_of,), jnp.float32, least / len(pieces), top_value / len(pieces))
        return jnp.repeat(jnp.exp(steps), dims[position] // shards_of).reshape((-1,) + (1,) * (len(dims) - position - 1))

    gain = one(*pieces[0])
    for cut in pieces[1:]:
        gain = gain * one(*cut)
    return gain


def gaussian(key, shape, deviation, bound, cuts=(), kind=jnp.bfloat16):
    factor_of = shard_levels(key, shape, cuts, -0.22, 0.18) if cuts else 1.0
    array = jax.random.normal(key, shape, jnp.float32) * deviation * factor_of
    return jnp.minimum(jnp.maximum(array, -bound), bound).astype(kind)


def setup_inputs(seed: int = 0) -> dict:
    key_of = jax.random.split(jax.random.key(seed), 4)
    sample = gaussian(key_of[0], (LEVELS, NROWS, SAMPLES), 1.0, 6.0, ((1, 256),), jnp.float32)
    probes = gaussian(key_of[1], (LEVELS, NROWS, SAMPLES), (NROWS // 8) ** -0.5, 0.03125, ((1, 256),), jnp.float32)
    skeleton_rows = draw_skeleton_rows(jax.random.fold_in(key_of[3], 71), 0)
    return {"sample": sample, "probes": probes, "skeleton_rows": skeleton_rows}


ridge_term = 0.05

def chol_solve(gram_matrix, right_side):
    factor = jnp.linalg.cholesky(gram_matrix)
    return jax.scipy.linalg.cho_solve((factor, True), right_side)

def exact_sum(form, left_side, right_side):
    return jnp.einsum(form, left_side, right_side, precision=lax.Precision.HIGHEST)

def pick_rows(block_rows, indices):
    return block_rows[indices]

def reference(sample, probes, skeleton_rows):
    row_total = sample.shape[1]
    identity = jnp.eye(SKEL, dtype=jnp.float32)
    bases = []
    couplings = []
    outputs = []
    for level_id in range(LEVELS):
        nodes = 2 ** (level_id + 1)
        node_rows = row_total // nodes
        corrected = sample[level_id].reshape(nodes, node_rows, SAMPLES)
        tests = probes[level_id].reshape(nodes, node_rows, SAMPLES)
        for coarse in range(level_id):
            coarse_nodes = 2 ** (coarse + 1)
            inner = nodes // coarse_nodes
            basis_here = bases[coarse].reshape(nodes, node_rows, SKEL)
            per_node = exact_sum('nrk,nrp->nkp', basis_here, tests)
            parity_slots = per_node.reshape(coarse_nodes, inner // 2, 2, SKEL, SAMPLES).sum(axis=1)
            swapped = parity_slots.reshape(coarse_nodes // 2, 2, 2, SKEL, SAMPLES)[:, ::-1]
            swapped = swapped.reshape(coarse_nodes, 2, SKEL, SAMPLES)
            owner = jnp.arange(nodes, dtype=jnp.int32) // inner
            parity = jnp.arange(nodes, dtype=jnp.int32) % 2
            chosen = swapped[owner, 1 - parity]
            mapped = exact_sum('nkj,njp->nkp', couplings[coarse][owner], chosen)
            corrected = corrected - exact_sum('nrk,nkp->nrp', basis_here, mapped)
        picked = skeleton_rows[nodes - 2:2 * nodes - 2]
        skeleton = jax.vmap(pick_rows)(corrected, picked)
        gram_matrix = exact_sum('nkp,njp->nkj', skeleton, skeleton) / SAMPLES + ridge_term * identity
        projected = exact_sum('nrp,nkp->nkr', corrected, skeleton) / SAMPLES
        basis_now = jnp.swapaxes(jax.vmap(chol_solve)(gram_matrix, projected), 1, 2)
        bases.append(basis_now.reshape(row_total, SKEL))
        moment = exact_sum('nrk,nrp->nkp', basis_now, tests)
        partner = moment.reshape(nodes // 2, 2, SKEL, SAMPLES)[:, ::-1].reshape(nodes, SKEL, SAMPLES)
        spread = exact_sum('nkp,njp->nkj', partner, partner) + ridge_term * identity
        cross = exact_sum('nkp,njp->nkj', partner, skeleton)
        coupled = jnp.swapaxes(jax.vmap(chol_solve)(spread, cross), 1, 2)
        couplings.append(coupled)
        outputs.append(jnp.repeat(coupled, GROUPS // nodes, axis=0))
    return (jnp.stack(bases), jnp.stack(outputs))
```

```python
import functools

import jax
import jax.numpy as jnp
from jax import lax
from jax.experimental import pallas as pl
from jax.experimental.pallas import tpu as pltpu
from jax.sharding import PartitionSpec as P

MESH = pl.DeviceIdType.MESH
F32 = jnp.float32
BF16 = jnp.bfloat16
ROWS = 896
SAMPLES = 512
SKEL = 128
RIDGE = 0.05
NROWS = 229376

HOPS = (0, 1, 2, 1)


def hops_of(d):
    return HOPS[d & 3] + (d >> 2 & 1) + (d >> 4 & 1)


PEERS = tuple(sorted(range(1, 32), key=lambda d: -hops_of(d)))
ROWMAJOR = (((1,), (0,)), ((), ()))
TRANSPOSED = (((1,), (1,)), ((), ()))


def split(x):
    hi = x.astype(BF16)
    return hi, (x - hi.astype(F32)).astype(BF16)


def dot(a, b, dims=ROWMAJOR):
    return lax.dot_general(a, b, dims, preferred_element_type=F32)


def exact(a, b, dims=ROWMAJOR):
    return lax.dot_general(a, b, dims, precision=lax.Precision.HIGHEST, preferred_element_type=F32)


def inverse(a):
    lane = lax.broadcasted_iota(jnp.int32, (8, 128), 1)
    sub = lax.broadcasted_iota(jnp.int32, (8, 128), 0)
    lane_rest = lax.broadcasted_iota(jnp.int32, (120, 128), 1)

    def body(_, a):
        p = a[0:8]
        c = [jnp.broadcast_to(p[:, i : i + 1], (8, 128)) for i in range(8)]
        for i in range(8):
            d = 1.0 / jnp.broadcast_to(c[i][i : i + 1], (8, 128))
            m = jnp.where(sub == i, 1.0 - d, c[i] * d)
            row = jnp.where(lane == i, 1.0, jnp.broadcast_to(p[i : i + 1], (8, 128)))
            z = jnp.where(lane == i, jnp.where(sub == i, 1.0, 0.0), p)
            p = z - m * row
            for j in range(i + 1, 8):
                c[j] = c[j] - m * jnp.broadcast_to(c[j][i : i + 1], (8, 128))
        r = a[8:]
        n = jnp.where(lane_rest < 8, 0.0, r)
        for i in range(8):
            n = n - r[:, i : i + 1] * p[i : i + 1]
        return pltpu.roll(jnp.concatenate([n, p], 0), 120, 1)

    return lax.fori_loop(0, 16, body, a)


def with_ridge(a, ridge):
    i = lax.broadcasted_iota(jnp.int32, (SKEL, SKEL), 0)
    j = lax.broadcasted_iota(jnp.int32, (SKEL, SKEL), 1)
    return a + jnp.where(i == j, ridge, 0.0)


def blocks_to_matrix(full):
    return jnp.concatenate([full[8 * c : 8 * c + 8].reshape(SKEL, 128) for c in range(4)], axis=1)


def kernel(
    rows_ref, sample_ref, probes_ref, basis_out, coupling_out,
    samp0, samp1, samp2, prob, sh, sl, pth, ptl, yref, basis, coup,
    st_a0, rs_a0, ex_a0, fu_a0,
    st_a1, rs_a1, ex_a1, fu_a1,
    st_b0, rs_b0, ex_b0, fu_b0,
    st_c0, rs_c0, ex_c0, exy_c0, fu_c0,
    st_b1, rs_b1, ex_b1, fu_b1,
    st_b2, rs_b2, ex_b2, fu_b2,
    red_a0, red_a1, red_b0, red_c0, red_b1, red_b2,
    ssem, rsem, insem, outsem,
):
    samp = (samp0, samp1, samp2)
    leaf = lax.axis_index("leaf")
    blk = lax.axis_index("blk")
    n2 = leaf // 4
    g = (leaf % 4) * 8 + blk
    leaf_step = [(1 - 2 * ((leaf // (1 << k)) % 2)) * (1 << k) for k in range(5)]
    blk_step = [(1 - 2 * ((blk // (1 << k)) % 2)) * (1 << k) for k in range(3)]

    def peer(d):
        a, b = leaf, blk
        for k in range(3):
            if d >> k & 1:
                b = b + blk_step[k]
        for k in range(2):
            if d >> (3 + k) & 1:
                a = a + leaf_step[k]
        return a, b

    def node(d):
        a = leaf
        for k in range(3):
            if d >> k & 1:
                a = a + leaf_step[2 + k]
        return a, blk

    loads = []
    for l in range(3):
        loads.append(pltpu.make_async_copy(sample_ref.at[l], samp[l], insem.at[l]))
    for l in range(3):
        loads.append(pltpu.make_async_copy(probes_ref.at[l], prob.at[l], insem.at[3 + l]))
    for c in loads:
        c.start()

    barrier = pltpu.get_barrier_semaphore()
    for d in PEERS:
        pl.semaphore_signal(barrier, inc=1, device_id=peer(d), device_id_type=MESH)
    for d in range(1, 8):
        pl.semaphore_signal(barrier, inc=1, device_id=node(d), device_id_type=MESH)

    def wait_bytes(ref, sem):
        pltpu.make_async_copy(ref, ref, sem).wait()

    def send(src, dst, stage, to):
        pltpu.make_async_remote_copy(
            src_ref=src, dst_ref=dst, send_sem=ssem.at[stage], recv_sem=rsem.at[stage],
            device_id=to, device_id_type=MESH,
        ).start()

    def scatter(st, rs, stage):
        for d in PEERS:
            a, b = peer(d)
            send(st.at[(a % 4) * 8 + b], rs.at[d - 1], stage, (a, b))

    def scattered(st, rs, stage):
        wait_bytes(rs, rsem.at[stage])
        return st[g] + jnp.sum(rs[...], axis=0)

    def gather(fu, stage):
        for d in PEERS:
            send(fu.at[g], fu.at[g], stage, peer(d))

    def gathered(fu, stage):
        wait_bytes(fu.at[pl.ds(1, 31)], rsem.at[stage])

    def pick(level, base, table_row, source, put):
        def one(i, _):
            at = rows_ref[table_row, i] + base
            own = (at >= 0) & (at < ROWS)
            safe = jnp.clip(at, 0, ROWS - 1)
            put(i, jnp.where(own, source(safe), 0.0))
            return 0

        lax.fori_loop(0, SKEL, one, 0, unroll=8)

    def table(level):
        node_id = leaf // (1 << (4 - level))
        base = node_id * (NROWS >> (level + 1)) - (leaf * 8 + blk) * ROWS
        return node_id + (2 ** (level + 1) - 2), base

    def pick_sample(level, st, offset):
        row, base = table(level)

        def put(i, v):
            for c in range(4):
                st[8 * c + i // 16, pl.ds(offset + i % 16, 1), :] = v[:, 128 * c : 128 * c + 128]

        pick(level, base, row, lambda at: samp[level][pl.ds(at, 1), :], put)

    def pick_y(level, st, first, offset):
        row, base = table(level)

        def put(i, v):
            st[first + i // 8, pl.ds(offset + i % 8, 1), :] = v

        pick(level, base, row, lambda at: yref[pl.ds(at, 1), :], put)

    def split_sample(l):
        hi, lo = split(samp[l][...])
        sh[l] = hi
        sl[l] = lo

    def split_probes(l):
        for i in range(7):
            t = prob[l, 128 * i : 128 * i + 128, :].T
            hi, lo = split(t)
            pth[l, :, 128 * i : 128 * i + 128] = hi
            ptl[l, :, 128 * i : 128 * i + 128] = lo

    def project(l, s):
        hi, lo = split(s)
        both = dot(sh[l], jnp.concatenate([hi, lo], axis=0), TRANSPOSED)
        return both[:, :SKEL] + both[:, SKEL:] + dot(sl[l], hi, TRANSPOSED)

    def test(l, yh, ycat):
        both = dot(pth[l], ycat)
        return both[:, :SKEL] + both[:, SKEL:] + dot(ptl[l], yh)

    def thin(a, b, dims=ROWMAJOR):
        ah, al = split(a)
        bh, bl = split(b)
        return dot(ah, bh, dims) + dot(ah, bl, dims) + dot(al, bh, dims)

    loads[0].wait()
    pick_sample(0, st_a0, 0)
    pl.semaphore_wait(barrier, 38)
    scatter(st_a0, rs_a0, 0)
    loads[1].wait()
    pick_sample(1, st_a1, 0)
    loads[2].wait()
    pick_sample(2, st_a1, 16)
    scatter(st_a1, rs_a1, 3)
    split_sample(0)
    red_a0[...] = scattered(st_a0, rs_a0, 0)
    for d in (1, 2, 3):
        send(red_a0, ex_a0.at[d - 1], 1, node(d))
    for c in loads[3:]:
        c.wait()
    split_probes(0)
    wait_bytes(ex_a0, rsem.at[1])
    fu_a0[g] = red_a0[...] + jnp.sum(ex_a0[...], axis=0)
    gather(fu_a0, 2)
    red_a1[...] = scattered(st_a1, rs_a1, 3)
    send(red_a1.at[pl.ds(0, 16)], ex_a1, 4, node(1))
    split_probes(1)
    split_probes(2)
    wait_bytes(ex_a1, rsem.at[4])
    fu_a1[g, 0:16] = red_a1[0:16] + ex_a1[...]
    fu_a1[g, 16:32] = red_a1[16:32]
    gathered(fu_a0, 2)
    gather(fu_a1, 5)

    s0 = blocks_to_matrix(fu_a0)
    y = project(0, s0)
    yref[...] = y
    yh, yl = split(y)
    ycat = jnp.concatenate([yh, yl], axis=1)
    st_b0[...] = test(0, yh, ycat).reshape(32, 16, 128)
    scatter(st_b0, rs_b0, 6)
    st_c0[:, 0:16] = test(1, yh, ycat).reshape(32, 16, 128)
    st_c0[:, 16:32] = test(2, yh, ycat).reshape(32, 16, 128)
    pick_y(1, st_c0, 0, 32)
    pick_y(2, st_c0, 16, 32)
    scatter(st_c0, rs_c0, 9)
    g0 = inverse(with_ridge(exact(s0, s0, TRANSPOSED), SAMPLES * RIDGE))
    red_b0[...] = exact(scattered(st_b0, rs_b0, 6), g0)
    for d in (4, 5, 6, 7):
        send(red_b0, ex_b0.at[d - 4], 7, node(d))
    basis[0] = thin(yref[...], g0)
    pltpu.make_async_copy(basis.at[0], basis_out.at[0], outsem.at[0]).start()
    split_sample(1)
    wait_bytes(ex_b0, rsem.at[7])
    fu_b0[g] = jnp.sum(ex_b0[...], axis=0)
    gather(fu_b0, 8)
    red_c0[...] = exact(scattered(st_c0, rs_c0, 9), g0)
    send(red_c0.at[pl.ds(0, 16)], ex_c0.at[pl.ds(32, 16)], 10, node(6))
    send(red_c0.at[pl.ds(0, 32)], ex_c0.at[pl.ds(0, 32)], 10, node(7))
    send(red_c0.at[pl.ds(16, 16)], ex_c0.at[pl.ds(48, 16)], 10, node(5))
    send(red_c0.at[pl.ds(32, 8)], exy_c0, 11, node(1))
    split_sample(2)
    wait_bytes(ex_c0, rsem.at[10])
    wait_bytes(exy_c0, rsem.at[11])
    fu_c0[g, 0:32] = ex_c0[0:32] + ex_c0[32:64]
    fu_c0[g, 32:40] = red_c0[32:40] + jnp.where(g < 16, exy_c0[...], 0.0)
    gathered(fu_b0, 8)
    gather(fu_c0, 12)

    def couple(s, mt):
        m = mt.T
        spread = inverse(with_ridge(exact(m, m, TRANSPOSED), RIDGE))
        return exact(exact(s, mt), spread)

    c0 = couple(s0, fu_b0[...].reshape(SAMPLES, SKEL))
    coup[0] = c0

    gathered(fu_a1, 5)
    gathered(fu_c0, 12)
    r1 = blocks_to_matrix(fu_a1[:, 0:16])
    b01 = fu_c0[0:16, 32:40].reshape(SKEL, SKEL)
    k1t = exact(fu_c0[:, 0:16].reshape(SAMPLES, SKEL), c0, TRANSPOSED)
    s1 = r1 - exact(b01, k1t, TRANSPOSED)
    y = project(1, s1) - thin(basis[0], exact(s1, k1t), TRANSPOSED)
    yref[...] = y
    yh, yl = split(y)
    ycat = jnp.concatenate([yh, yl], axis=1)
    st_b1[:, 0:16] = test(1, yh, ycat).reshape(32, 16, 128)
    st_b1[:, 16:32] = test(2, yh, ycat).reshape(32, 16, 128)
    pick_y(2, st_b1, 0, 32)
    st_b1[16:32, 32:40] = jnp.zeros((16, 8, 128), F32)
    scatter(st_b1, rs_b1, 13)
    g1 = inverse(with_ridge(exact(s1, s1, TRANSPOSED), SAMPLES * RIDGE))
    red_b1[...] = exact(scattered(st_b1, rs_b1, 13), g1)
    send(red_b1.at[pl.ds(0, 32)], ex_b1.at[pl.ds(0, 32)], 14, node(3))
    send(red_b1.at[pl.ds(0, 16)], ex_b1.at[pl.ds(32, 16)], 14, node(2))
    basis[1] = thin(yref[...], g1)
    pltpu.make_async_copy(basis.at[1], basis_out.at[1], outsem.at[1]).start()
    b02 = fu_c0[16:32, 32:40].reshape(SKEL, SKEL)
    k2t = exact(fu_c0[:, 16:32].reshape(SAMPLES, SKEL), c0, TRANSPOSED)
    part2 = blocks_to_matrix(fu_a1[:, 16:32]) - exact(b02, k2t, TRANSPOSED)
    wait_bytes(ex_b1, rsem.at[14])
    fu_b1[g, 0:16] = ex_b1[0:16] + ex_b1[32:48]
    fu_b1[g, 16:32] = ex_b1[16:32]
    fu_b1[g, 32:40] = red_b1[32:40]
    gather(fu_b1, 15)
    gathered(fu_b1, 15)
    c1 = couple(s1, fu_b1[:, 0:16].reshape(SAMPLES, SKEL))
    coup[1] = c1

    b12 = fu_b1[0:16, 32:40].reshape(SKEL, SKEL)
    k3t = exact(fu_b1[:, 16:32].reshape(SAMPLES, SKEL), c1, TRANSPOSED)
    s2 = part2 - exact(b12, k3t, TRANSPOSED)
    y = project(2, s2) - thin(basis[0], exact(s2, k2t), TRANSPOSED) - thin(basis[1], exact(s2, k3t), TRANSPOSED)
    yref[...] = y
    yh, yl = split(y)
    ycat = jnp.concatenate([yh, yl], axis=1)
    st_b2[...] = test(2, yh, ycat).reshape(32, 16, 128)
    scatter(st_b2, rs_b2, 16)
    g2 = inverse(with_ridge(exact(s2, s2, TRANSPOSED), SAMPLES * RIDGE))
    red_b2[...] = exact(scattered(st_b2, rs_b2, 16), g2)
    send(red_b2, ex_b2, 17, node(1))
    basis[2] = thin(yref[...], g2)
    pltpu.make_async_copy(basis.at[2], basis_out.at[2], outsem.at[2]).start()
    wait_bytes(ex_b2, rsem.at[17])
    fu_b2[g] = ex_b2[...]
    gather(fu_b2, 18)
    gathered(fu_b2, 18)
    coup[2] = couple(s2, fu_b2[...].reshape(SAMPLES, SKEL))
    pltpu.make_async_copy(coup, coupling_out, outsem.at[3]).start()

    for rs, stage in ((rs_a0, 0), (rs_a1, 3), (rs_b0, 6), (rs_c0, 9), (rs_b1, 13), (rs_b2, 16)):
        wait_bytes(rs, ssem.at[stage])
    for fu, stage in ((fu_a0, 2), (fu_a1, 5), (fu_b0, 8), (fu_c0, 12), (fu_b1, 15), (fu_b2, 18)):
        wait_bytes(fu.at[pl.ds(1, 31)], ssem.at[stage])
    for ex, stage in ((ex_a0, 1), (ex_a1, 4), (ex_b0, 7), (ex_c0, 10), (exy_c0, 11), (ex_b1, 14), (ex_b2, 17)):
        wait_bytes(ex, ssem.at[stage])
    for l in range(3):
        pltpu.make_async_copy(basis.at[l], basis_out.at[l], outsem.at[l]).wait()
    pltpu.make_async_copy(coup, coupling_out, outsem.at[3]).wait()


def vm(*shape, dtype=F32):
    return pltpu.VMEM(shape, dtype)


def local(sample, probes, skeleton_rows):
    def quad(rows, ex):
        return [vm(32, rows, 128), vm(31, rows, 128)] + ex + [vm(32, rows, 128)]

    scratch = [
        vm(ROWS, SAMPLES), vm(ROWS, SAMPLES), vm(ROWS, SAMPLES), vm(3, ROWS, SAMPLES),
        vm(3, ROWS, SAMPLES, dtype=BF16), vm(3, ROWS, SAMPLES, dtype=BF16),
        vm(3, SAMPLES, ROWS, dtype=BF16), vm(3, SAMPLES, ROWS, dtype=BF16),
        vm(ROWS, SKEL), vm(3, ROWS, SKEL), vm(3, SKEL, SKEL),
        *quad(16, [vm(3, 16, 128)]),
        *quad(32, [vm(16, 128)]),
        *quad(16, [vm(4, 16, 128)]),
        *quad(40, [vm(64, 128), vm(8, 128)]),
        *quad(40, [vm(48, 128)]),
        *quad(16, [vm(16, 128)]),
        vm(16, 128), vm(32, 128), vm(16, 128), vm(40, 128), vm(40, 128), vm(16, 128),
        pltpu.SemaphoreType.DMA((19,)), pltpu.SemaphoreType.DMA((19,)),
        pltpu.SemaphoreType.DMA((6,)), pltpu.SemaphoreType.DMA((4,)),
    ]
    basis, coupling = pl.pallas_call(
        kernel,
        out_shape=(
            jax.ShapeDtypeStruct((3, ROWS, SKEL), F32),
            jax.ShapeDtypeStruct((3, SKEL, SKEL), F32),
        ),
        in_specs=[
            pl.BlockSpec(memory_space=pltpu.SMEM),
            pl.BlockSpec(memory_space=pl.ANY),
            pl.BlockSpec(memory_space=pl.ANY),
        ],
        out_specs=(pl.BlockSpec(memory_space=pl.ANY), pl.BlockSpec(memory_space=pl.ANY)),
        scratch_shapes=scratch,
        compiler_params=pltpu.CompilerParams(
            collective_id=0, has_side_effects=True, vmem_limit_bytes=52 * 2**20
        ),
    )(skeleton_rows, sample, probes)
    return basis, coupling[:, None]


def solution(mesh):
    placed = (P(None, ("leaf", "blk"), None), P(None, ("leaf", "blk"), None), P())
    return jax.shard_map(
        local,
        mesh=mesh,
        in_specs=placed,
        out_specs=(P(None, ("leaf", "blk"), None), P(None, "leaf", None, None)),
        check_vma=False,
    )
```

```python
import functools

import jax
import jax.numpy as jnp
from jax import lax
from jax.experimental import pallas as pl
from jax.experimental.pallas import tpu as pltpu
from jax.sharding import PartitionSpec as P

MESH = pl.DeviceIdType.MESH
F32 = jnp.float32
BF16 = jnp.bfloat16
ROWS = 896
SAMPLES = 512
SKEL = 128
RIDGE = 0.05
NROWS = 229376

STEP = 16

HOPS = (0, 1, 2, 1)


def far(mask):
    a, b = mask
    return HOPS[a >> 1 & 3] + HOPS[b & 3] + (b >> 2)


def masks(first, leaf_bits, blk_bits):
    every = [(first + a, b) for a in range(1 << leaf_bits) for b in range(1 << blk_bits)]
    return tuple(sorted((m for m in every if m != (0, 0)), key=lambda m: -far(m)))


NODE = masks(0, 2, 3)
PLANE = masks(0, 3, 2)
SIBLING = masks(4, 2, 3)
HALF = ((0, 4), (8, 0), (8, 4))
ACROSS = ((16, 0), (16, 4), (24, 0), (24, 4))
OTHERS = HALF + ACROSS + ((20, 0), (28, 0), (12, 0))
ALL = tuple(dict.fromkeys(SIBLING + NODE + PLANE + OTHERS))

ROWMAJOR = (((1,), (0,)), ((), ()))
TRANSPOSED = (((1,), (1,)), ((), ()))


def split(x):
    hi = x.astype(BF16)
    return hi, (x - hi.astype(F32)).astype(BF16)


def dot(a, b, dims=ROWMAJOR):
    return lax.dot_general(a, b, dims, preferred_element_type=F32)


def exact(a, b, dims=ROWMAJOR):
    return lax.dot_general(a, b, dims, precision=lax.Precision.HIGHEST, preferred_element_type=F32)


def inverse(a):
    lane = lax.broadcasted_iota(jnp.int32, (STEP, 128), 1)
    sub = lax.broadcasted_iota(jnp.int32, (STEP, 128), 0)
    lane_rest = lax.broadcasted_iota(jnp.int32, (128 - STEP, 128), 1)

    def body(_, a):
        p = a[0:STEP]
        c = [jnp.broadcast_to(p[:, i : i + 1], (STEP, 128)) for i in range(STEP)]
        for i in range(STEP):
            d = 1.0 / jnp.broadcast_to(c[i][i : i + 1], (STEP, 128))
            m = jnp.where(sub == i, 1.0 - d, c[i] * d)
            row = jnp.where(lane == i, 1.0, jnp.broadcast_to(p[i : i + 1], (STEP, 128)))
            z = jnp.where(lane == i, jnp.where(sub == i, 1.0, 0.0), p)
            p = z - m * row
            for j in range(i + 1, STEP):
                c[j] = c[j] - m * jnp.broadcast_to(c[j][i : i + 1], (STEP, 128))
        r = a[STEP:]
        n = jnp.where(lane_rest < STEP, 0.0, r)
        for i in range(STEP):
            n = n - r[:, i : i + 1] * p[i : i + 1]
        return pltpu.roll(jnp.concatenate([n, p], 0), 128 - STEP, 1)

    return lax.fori_loop(0, 128 // STEP, body, a)


def with_ridge(a, ridge):
    i = lax.broadcasted_iota(jnp.int32, (SKEL, SKEL), 0)
    j = lax.broadcasted_iota(jnp.int32, (SKEL, SKEL), 1)
    return a + jnp.where(i == j, ridge, 0.0)


def blocks_to_matrix(full):
    return jnp.concatenate([full[8 * c : 8 * c + 8].reshape(SKEL, 128) for c in range(4)], axis=1)


def kernel(
    rows_ref, sample_ref, probes_ref, basis_out, coupling_out,
    samp0, samp1, samp2, prob, sh, sl, pth, ptl, yref, basis, coup,
    st_a0, rs_a0, ex_a0, fu_a0, red_a0,
    st_a1, rs_a1, ex_a1, fu_a1, red_a1,
    st_b0, rs_b0, ex_b0, fu_b0, red_b0,
    st_c0, rs_c0, ex_c0, exy_c0, fu_c0, red_c0,
    st_d0, rs_d0, ex_d0, fu_d0, red_d0,
    st_b1, rs_b1, ex_b1, fu_b1, red_b1,
    st_d1, rs_d1, ex_d1, fu_d1, red_d1,
    st_b2, rs_b2, ex_b2, fu_b2, red_b2,
    ssem, rsem, insem, outsem,
):
    samp = (samp0, samp1, samp2)
    leaf = lax.axis_index("leaf")
    blk = lax.axis_index("blk")
    leaf_step = [(1 - 2 * ((leaf // (1 << k)) % 2)) * (1 << k) for k in range(5)]
    blk_step = [(1 - 2 * ((blk // (1 << k)) % 2)) * (1 << k) for k in range(3)]

    def at(mask):
        a, b = leaf, blk
        for k in range(5):
            if mask[0] >> k & 1:
                a = a + leaf_step[k]
        for k in range(3):
            if mask[1] >> k & 1:
                b = b + blk_step[k]
        return a, b

    def in_node(a, b):
        return (a % 4) * 8 + b

    def in_plane(a, b):
        return (a % 8) * 4 + b % 4

    gn = in_node(leaf, blk)
    gp = in_plane(leaf, blk)

    loads = {}
    for l in range(3):
        loads[l] = pltpu.make_async_copy(sample_ref.at[l], samp[l], insem.at[l])
    for l in range(3):
        loads[3 + l] = pltpu.make_async_copy(probes_ref.at[l], prob.at[l], insem.at[3 + l])
    for c in loads.values():
        c.start()

    barrier = pltpu.get_barrier_semaphore()
    for m in ALL:
        pl.semaphore_signal(barrier, inc=1, device_id=at(m), device_id_type=MESH)

    leaving, landing, writing = [], {}, []

    def wait_bytes(ref, sem):
        pltpu.make_async_copy(ref, ref, sem).wait()

    def start(ref, stage):
        leaving.append((ref, stage))
        landing[stage] = ref

    def arrive(stage):
        wait_bytes(landing.pop(stage), rsem.at[stage])

    def write(src, dst, i):
        copy = pltpu.make_async_copy(src, dst, outsem.at[i])
        copy.start()
        writing.append(copy)

    def finish():
        for copy in loads.values():
            copy.wait()
        for stage in tuple(landing):
            arrive(stage)
        for ref, stage in leaving:
            wait_bytes(ref, ssem.at[stage])
        for copy in writing:
            copy.wait()

    def send(src, dst, stage, to):
        pltpu.make_async_remote_copy(
            src_ref=src, dst_ref=dst, send_sem=ssem.at[stage], recv_sem=rsem.at[stage],
            device_id=to, device_id_type=MESH,
        ).start()

    def scatter(st, rs, stage, group, number):
        for i, m in enumerate(group):
            to = at(m)
            send(st.at[number(*to)], rs.at[i], stage, to)
        start(rs, stage)

    def exchange(pieces, ex, stage):
        for src, dst, m in pieces:
            send(src, dst, stage, at(m))
        start(ex, stage)

    def gather(fu, stage, group, mine):
        for m in group:
            send(fu.at[mine], fu.at[mine], stage, at(m))
        start(fu.at[pl.ds(1, 31)], stage)

    def pick(level, base, table_row, source, put):
        def one(i, _):
            place = rows_ref[table_row, i] + base
            own = (place >= 0) & (place < ROWS)
            safe = jnp.clip(place, 0, ROWS - 1)
            put(i, jnp.where(own, source(safe), 0.0))
            return 0

        lax.fori_loop(0, SKEL, one, 0, unroll=8)

    def table(level):
        node_id = leaf // (1 << (4 - level))
        base = node_id * (NROWS >> (level + 1)) - (leaf * 8 + blk) * ROWS
        return node_id + (2 ** (level + 1) - 2), base

    def pick_sample(level, st, offset):
        row, base = table(level)

        def put(i, v):
            for c in range(4):
                st[8 * c + i // 16, pl.ds(offset + i % 16, 1), :] = v[:, 128 * c : 128 * c + 128]

        pick(level, base, row, lambda i: samp[level][pl.ds(i, 1), :], put)

    def pick_y(level, st, offset):
        row, base = table(level)

        def put(i, v):
            st[i // 8, pl.ds(offset + i % 8, 1), :] = v

        pick(level, base, row, lambda i: yref[pl.ds(i, 1), :], put)
        st[16:32, offset : offset + 8] = jnp.zeros((16, 8, 128), F32)

    def split_sample(l):
        hi, lo = split(samp[l][...])
        sh[l] = hi
        sl[l] = lo

    def split_probes(l):
        for i in range(7):
            t = prob[l, 128 * i : 128 * i + 128, :].T
            hi, lo = split(t)
            pth[l, :, 128 * i : 128 * i + 128] = hi
            ptl[l, :, 128 * i : 128 * i + 128] = lo

    def project(l, s):
        hi, lo = split(s)
        both = dot(sh[l], jnp.concatenate([hi, lo], axis=0), TRANSPOSED)
        return both[:, :SKEL] + both[:, SKEL:] + dot(sl[l], hi, TRANSPOSED)

    def test(l, yh, ycat):
        both = dot(pth[l], ycat)
        return both[:, :SKEL] + both[:, SKEL:] + dot(ptl[l], yh)

    def thin(a, b, dims=ROWMAJOR):
        ah, al = split(a)
        bh, bl = split(b)
        return dot(ah, bh, dims) + dot(ah, bl, dims) + dot(al, bh, dims)

    def couple(s, mt):
        m = mt.T
        spread = inverse(with_ridge(exact(m, m, TRANSPOSED), RIDGE))
        return exact(exact(s, mt), spread)

    def gram_inverse(s):
        return inverse(with_ridge(exact(s, s, TRANSPOSED), SAMPLES * RIDGE))

    loads.pop(0).wait()
    pick_sample(0, st_a0, 0)
    pl.semaphore_wait(barrier, len(ALL))
    scatter(st_a0, rs_a0, 0, PLANE, in_plane)
    loads.pop(1).wait()
    pick_sample(1, st_a1, 0)
    scatter(st_a1, rs_a1, 3, PLANE, in_plane)
    split_sample(0)
    arrive(0)
    red_a0[...] = st_a0[gp] + jnp.sum(rs_a0[...], axis=0)
    exchange([(red_a0, ex_a0.at[i], m) for i, m in enumerate(HALF)], ex_a0, 1)
    loads.pop(3).wait()
    split_probes(0)
    arrive(3)
    red_a1[...] = st_a1[gp] + jnp.sum(rs_a1[...], axis=0)
    arrive(1)
    fu_a0[gp] = red_a0[...] + jnp.sum(ex_a0[...], axis=0)
    gather(fu_a0, 2, PLANE, gp)
    exchange([(red_a1, ex_a1, (0, 4))], ex_a1, 4)
    loads.pop(2).wait()
    pick_sample(2, st_d0, 24)
    loads.pop(4).wait()
    split_probes(1)
    loads.pop(5).wait()
    split_probes(2)
    arrive(4)
    fu_a1[gp] = red_a1[...] + ex_a1[...]
    gather(fu_a1, 5, PLANE, gp)

    arrive(2)
    s0 = blocks_to_matrix(fu_a0)
    y = project(0, s0)
    yref[...] = y
    yh, yl = split(y)
    ycat = jnp.concatenate([yh, yl], axis=1)
    st_b0[...] = test(0, yh, ycat).reshape(32, 16, 128)
    scatter(st_b0, rs_b0, 6, PLANE, in_plane)
    st_c0[:, 0:16] = test(1, yh, ycat).reshape(32, 16, 128)
    pick_y(1, st_c0, 16)
    scatter(st_c0, rs_c0, 9, PLANE, in_plane)
    g0 = gram_inverse(s0)
    arrive(6)
    red_b0[...] = exact(st_b0[gp] + jnp.sum(rs_b0[...], axis=0), g0)
    exchange([(red_b0, ex_b0.at[i], m) for i, m in enumerate(ACROSS)], ex_b0, 7)
    arrive(9)
    red_c0[...] = exact(st_c0[gp] + jnp.sum(rs_c0[...], axis=0), g0)
    exchange([(red_c0.at[pl.ds(0, 16)], ex_c0.at[i], m) for i, m in enumerate(ACROSS[2:])], ex_c0, 10)
    exchange([(red_c0.at[pl.ds(16, 8)], exy_c0, (0, 4))], exy_c0, 11)
    st_d0[:, 0:16] = test(2, yh, ycat).reshape(32, 16, 128)
    pick_y(2, st_d0, 16)
    arrive(7)
    fu_b0[gp] = jnp.sum(ex_b0[...], axis=0)
    gather(fu_b0, 8, PLANE, gp)
    arrive(10)
    arrive(11)
    fu_c0[gp, 0:16] = jnp.sum(ex_c0[...], axis=0)
    fu_c0[gp, 16:24] = red_c0[16:24] + exy_c0[...]
    gather(fu_c0, 12, PLANE, gp)
    basis[0] = thin(yref[...], g0)
    write(basis.at[0], basis_out.at[0], 0)
    split_sample(1)
    arrive(8)
    scatter(st_d0, rs_d0, 13, NODE, in_node)
    c0 = couple(s0, fu_b0[...].reshape(SAMPLES, SKEL))
    coup[0] = c0

    arrive(5)
    arrive(12)
    k1t = exact(fu_c0[:, 0:16].reshape(SAMPLES, SKEL), c0, TRANSPOSED)
    s1 = blocks_to_matrix(fu_a1) - exact(fu_c0[0:16, 16:24].reshape(SKEL, SKEL), k1t, TRANSPOSED)
    y = project(1, s1) - thin(basis[0], exact(s1, k1t), TRANSPOSED)
    yref[...] = y
    yh, yl = split(y)
    ycat = jnp.concatenate([yh, yl], axis=1)
    st_b1[...] = test(1, yh, ycat).reshape(32, 16, 128)
    scatter(st_b1, rs_b1, 16, PLANE, in_plane)
    st_d1[:, 0:16] = test(2, yh, ycat).reshape(32, 16, 128)
    pick_y(2, st_d1, 16)
    scatter(st_d1, rs_d1, 19, NODE, in_node)
    arrive(13)
    sum_d0 = st_d0[gn] + jnp.sum(rs_d0[...], axis=0)
    red_d0[0:24] = exact(sum_d0[0:24], g0)
    red_d0[24:40] = sum_d0[24:40]
    exchange([(red_d0.at[pl.ds(0, 16)], ex_d0.at[i], m) for i, m in enumerate(((20, 0), (28, 0)))], ex_d0, 14)
    g1 = gram_inverse(s1)
    arrive(16)
    red_b1[...] = exact(st_b1[gp] + jnp.sum(rs_b1[...], axis=0), g1)
    exchange([(red_b1, ex_b1.at[i], m) for i, m in enumerate(((8, 0), (8, 4)))], ex_b1, 17)
    arrive(19)
    red_d1[...] = exact(st_d1[gn] + jnp.sum(rs_d1[...], axis=0), g1)
    exchange([(red_d1.at[pl.ds(0, 16)], ex_d1, (12, 0))], ex_d1, 20)
    arrive(17)
    fu_b1[gp] = jnp.sum(ex_b1[...], axis=0)
    gather(fu_b1, 18, PLANE, gp)
    arrive(20)
    fu_d1[gn, 0:16] = ex_d1[...]
    fu_d1[gn, 16:24] = red_d1[16:24]
    gather(fu_d1, 21, NODE, gn)
    arrive(14)
    fu_d0[gn, 0:16] = jnp.sum(ex_d0[...], axis=0)
    fu_d0[gn, 16:40] = red_d0[16:40]
    gather(fu_d0, 15, NODE, gn)
    basis[1] = thin(yref[...], g1)
    write(basis.at[1], basis_out.at[1], 1)
    split_sample(2)
    arrive(18)
    c1 = couple(s1, fu_b1[...].reshape(SAMPLES, SKEL))
    coup[1] = c1

    arrive(15)
    k2t = exact(fu_d0[:, 0:16].reshape(SAMPLES, SKEL), c0, TRANSPOSED)
    part2 = blocks_to_matrix(fu_d0[:, 24:40]) - exact(fu_d0[0:16, 16:24].reshape(SKEL, SKEL), k2t, TRANSPOSED)
    arrive(21)
    k3t = exact(fu_d1[:, 0:16].reshape(SAMPLES, SKEL), c1, TRANSPOSED)
    s2 = part2 - exact(fu_d1[0:16, 16:24].reshape(SKEL, SKEL), k3t, TRANSPOSED)
    y = project(2, s2) - thin(basis[0], exact(s2, k2t), TRANSPOSED) - thin(basis[1], exact(s2, k3t), TRANSPOSED)
    yref[...] = y
    yh, yl = split(y)
    ycat = jnp.concatenate([yh, yl], axis=1)
    st_b2[...] = test(2, yh, ycat).reshape(32, 16, 128)
    scatter(st_b2, rs_b2, 22, SIBLING, in_node)
    red_b2[...] = gram_inverse(s2)
    exchange([(red_b2, ex_b2, (4, 0))], ex_b2, 23)
    arrive(22)
    fu_b2[gn] = jnp.sum(rs_b2[...], axis=0)
    gather(fu_b2, 24, NODE, gn)
    basis[2] = thin(yref[...], red_b2[...])
    write(basis.at[2], basis_out.at[2], 2)
    arrive(23)
    arrive(24)
    coup[2] = couple(s2, exact(fu_b2[...].reshape(SAMPLES, SKEL), ex_b2[...]))
    write(coup, coupling_out, 3)

    finish()


def vm(*shape, dtype=F32):
    return pltpu.VMEM(shape, dtype)


def local(sample, probes, skeleton_rows):
    def phase(rows, ex, received=31):
        return [vm(32, rows, 128), vm(received, rows, 128), *ex, vm(32, rows, 128), vm(rows, 128)]

    scratch = [
        vm(ROWS, SAMPLES), vm(ROWS, SAMPLES), vm(ROWS, SAMPLES), vm(3, ROWS, SAMPLES),
        vm(3, ROWS, SAMPLES, dtype=BF16), vm(3, ROWS, SAMPLES, dtype=BF16),
        vm(3, SAMPLES, ROWS, dtype=BF16), vm(3, SAMPLES, ROWS, dtype=BF16),
        vm(ROWS, SKEL), vm(3, ROWS, SKEL), vm(3, SKEL, SKEL),
        *phase(16, [vm(3, 16, 128)]),
        *phase(16, [vm(16, 128)]),
        *phase(16, [vm(4, 16, 128)]),
        *phase(24, [vm(2, 16, 128), vm(8, 128)]),
        *phase(40, [vm(2, 16, 128)]),
        *phase(16, [vm(2, 16, 128)]),
        *phase(24, [vm(16, 128)]),
        vm(32, 16, 128), vm(32, 16, 128), vm(SKEL, SKEL), vm(32, 16, 128), vm(SKEL, SKEL),
        pltpu.SemaphoreType.DMA((25,)), pltpu.SemaphoreType.DMA((25,)),
        pltpu.SemaphoreType.DMA((6,)), pltpu.SemaphoreType.DMA((4,)),
    ]
    basis, coupling = pl.pallas_call(
        kernel,
        out_shape=(
            jax.ShapeDtypeStruct((3, ROWS, SKEL), F32),
            jax.ShapeDtypeStruct((3, SKEL, SKEL), F32),
        ),
        in_specs=[
            pl.BlockSpec(memory_space=pltpu.SMEM),
            pl.BlockSpec(memory_space=pl.ANY),
            pl.BlockSpec(memory_space=pl.ANY),
        ],
        out_specs=(pl.BlockSpec(memory_space=pl.ANY), pl.BlockSpec(memory_space=pl.ANY)),
        scratch_shapes=scratch,
        compiler_params=pltpu.CompilerParams(
            collective_id=0, has_side_effects=True, vmem_limit_bytes=52 * 2**20
        ),
    )(skeleton_rows, sample, probes)
    return basis, coupling[:, None]


def solution(mesh):
    placed = (P(None, ("leaf", "blk"), None), P(None, ("leaf", "blk"), None), P())
    return jax.shard_map(
        local,
        mesh=mesh,
        in_specs=placed,
        out_specs=(P(None, ("leaf", "blk"), None), P(None, "leaf", None, None)),
        check_vma=False,
    )
```

```python
import functools

import jax
import jax.numpy as jnp
from jax import lax
from jax.experimental import pallas as pl
from jax.experimental.pallas import tpu as pltpu
from jax.sharding import PartitionSpec as P

MESH = pl.DeviceIdType.MESH
F32 = jnp.float32
BF16 = jnp.bfloat16
ROWS = 896
SAMPLES = 512
SKEL = 128
RIDGE = 0.05
NROWS = 229376

STEP = 16
A0, A1, B0, C0, D0, B1, D1, B2 = range(0, 48, 6)

HOPS = (0, 1, 2, 1)
CORE = (1, 0)


def far(mask):
    a, b = mask
    return HOPS[a >> 1 & 3] + HOPS[b & 3] + (b >> 2)


def masks(leaf_masks, blk_masks):
    every = [(a, b) for a in leaf_masks for b in range(blk_masks)]
    return tuple(sorted((m for m in every if m != (0, 0)), key=lambda m: -far(m)))


NODE = masks((0, 2), 8)
PLANE = masks((0, 2, 4, 6), 4)
SIBLING = masks((4, 6), 8)
HALF = ((0, 4), (8, 0), (8, 4))
ACROSS = ((16, 0), (16, 4), (24, 0), (24, 4))
ALL = tuple(dict.fromkeys(ACROSS + ((12, 0),) + SIBLING + HALF + PLANE + NODE + (CORE,)))

ROWMAJOR = (((1,), (0,)), ((), ()))
TRANSPOSED = (((1,), (1,)), ((), ()))


def split(x):
    hi = x.astype(BF16)
    return hi, (x - hi.astype(F32)).astype(BF16)


def dot(a, b, dims=ROWMAJOR):
    return lax.dot_general(a, b, dims, preferred_element_type=F32)


def exact(a, b, dims=ROWMAJOR):
    return lax.dot_general(a, b, dims, precision=lax.Precision.HIGHEST, preferred_element_type=F32)


def inverse(a):
    lane = lax.broadcasted_iota(jnp.int32, (STEP, 128), 1)
    sub = lax.broadcasted_iota(jnp.int32, (STEP, 128), 0)
    lane_rest = lax.broadcasted_iota(jnp.int32, (128 - STEP, 128), 1)

    def body(_, a):
        p = a[0:STEP]
        c = [jnp.broadcast_to(p[:, i : i + 1], (STEP, 128)) for i in range(STEP)]
        for i in range(STEP):
            d = 1.0 / jnp.broadcast_to(c[i][i : i + 1], (STEP, 128))
            m = jnp.where(sub == i, 1.0 - d, c[i] * d)
            row = jnp.where(lane == i, 1.0, jnp.broadcast_to(p[i : i + 1], (STEP, 128)))
            z = jnp.where(lane == i, jnp.where(sub == i, 1.0, 0.0), p)
            p = z - m * row
            for j in range(i + 1, STEP):
                c[j] = c[j] - m * jnp.broadcast_to(c[j][i : i + 1], (STEP, 128))
        r = a[STEP:]
        n = jnp.where(lane_rest < STEP, 0.0, r)
        for i in range(STEP):
            n = n - r[:, i : i + 1] * p[i : i + 1]
        return pltpu.roll(jnp.concatenate([n, p], 0), 128 - STEP, 1)

    return lax.fori_loop(0, 128 // STEP, body, a)


def with_ridge(a, ridge):
    i = lax.broadcasted_iota(jnp.int32, (SKEL, SKEL), 0)
    j = lax.broadcasted_iota(jnp.int32, (SKEL, SKEL), 1)
    return a + jnp.where(i == j, ridge, 0.0)


def blocks_to_matrix(full):
    return jnp.concatenate([full[8 * c : 8 * c + 8].reshape(SKEL, 128) for c in range(4)], axis=1)


def kernel(
    rows_ref, sample_ref, probes_ref, basis_out, coupling_out,
    samp0, samp1, samp2, prob, sh, sl, pth, ptl, yref, basis, coup,
    st_a0, co_a0, rs_a0, ex_a0, fu_a0, red_a0,
    st_a1, co_a1, rs_a1, ex_a1, fu_a1, red_a1,
    st_b0, co_b0, rs_b0, ex_b0, fu_b0, red_b0,
    st_c0, co_c0, rs_c0, ex_c0, exy_c0, fu_c0, red_c0,
    st_d0, co_d0, rs_d0, ex_d0, exy_d0, fu_d0, red_d0, swap_d0,
    st_b1, co_b1, rs_b1, ex_b1, fu_b1, red_b1,
    st_d1, co_d1, rs_d1, ex_d1, fu_d1, red_d1,
    st_b2, co_b2, rs_b2, ex_b2, fu_b2, red_b2,
    ssem, rsem, insem, outsem,
):
    samp = (samp0, samp1, samp2)
    leaf = lax.axis_index("leaf")
    blk = lax.axis_index("blk")
    leaf_step = [(1 - 2 * ((leaf // (1 << k)) % 2)) * (1 << k) for k in range(5)]
    blk_step = [(1 - 2 * ((blk // (1 << k)) % 2)) * (1 << k) for k in range(3)]

    def at(mask):
        a, b = leaf, blk
        for k in range(5):
            if mask[0] >> k & 1:
                a = a + leaf_step[k]
        for k in range(3):
            if mask[1] >> k & 1:
                b = b + blk_step[k]
        return a, b

    core = leaf % 2
    own = pl.ds(16 * core, 16)
    other = pl.ds(16 * (1 - core), 16)

    def in_node(a, b):
        return (a % 2) * 16 + (a // 2 % 2) * 8 + b

    def in_plane(a, b):
        return (a % 2) * 16 + (a // 2 % 4) * 4 + b % 4

    gn = in_node(leaf, blk)
    gp = in_plane(leaf, blk)

    loads = {}
    for l in range(3):
        loads[l] = pltpu.make_async_copy(sample_ref.at[l], samp[l], insem.at[l])
    for l in range(3):
        loads[3 + l] = pltpu.make_async_copy(probes_ref.at[l], prob.at[l], insem.at[3 + l])
    for c in loads.values():
        c.start()

    barrier = pltpu.get_barrier_semaphore()
    for m in ALL:
        pl.semaphore_signal(barrier, inc=1, device_id=at(m), device_id_type=MESH)

    leaving, landing, writing = [], {}, []

    def wait_bytes(ref, sem):
        pltpu.make_async_copy(ref, ref, sem).wait()

    def start(ref, stage):
        leaving.append((ref, stage))
        landing[stage] = ref

    def arrive(stage):
        wait_bytes(landing.pop(stage), rsem.at[stage])

    def write(src, dst, i):
        copy = pltpu.make_async_copy(src, dst, outsem.at[i])
        copy.start()
        writing.append(copy)

    def finish():
        for copy in loads.values():
            copy.wait()
        for stage in tuple(landing):
            arrive(stage)
        for ref, stage in leaving:
            wait_bytes(ref, ssem.at[stage])
        for copy in writing:
            copy.wait()

    def send(src, dst, stage, to):
        pltpu.make_async_remote_copy(
            src_ref=src, dst_ref=dst, send_sem=ssem.at[stage], recv_sem=rsem.at[stage],
            device_id=to, device_id_type=MESH,
        ).start()

    def share(st, co, stage):
        send(st.at[other], co, stage, at(CORE))
        start(co, stage)

    def scatter(st, co, rs, stage, group, number):
        arrive(stage)
        st[own] = st[own] + co[...]
        for i, m in enumerate(group):
            to = at(m)
            send(st.at[number(*to)], rs.at[i], stage + 1, to)
        start(rs, stage + 1)

    def exchange(pieces, ex, stage):
        for src, dst, m in pieces:
            send(src, dst, stage, at(m))
        start(ex, stage)

    def gather(fu, stage, group, mine):
        for m in group:
            send(fu.at[mine], fu.at[mine], stage, at(m))
        start(fu.at[pl.ds(0, 15)], stage)

    def forward(fu, stage):
        arrive(stage)
        send(fu.at[own], fu.at[own], stage + 1, at(CORE))
        start(fu.at[other], stage + 1)

    def pick(level, base, table_row, source, put):
        def one(i, _):
            place = rows_ref[table_row, i] + base
            here = (place >= 0) & (place < ROWS)
            safe = jnp.clip(place, 0, ROWS - 1)
            put(i, jnp.where(here, source(safe), 0.0))
            return 0

        lax.fori_loop(0, SKEL, one, 0, unroll=8)

    def table(level):
        node_id = leaf // (1 << (4 - level))
        base = node_id * (NROWS >> (level + 1)) - (leaf * 8 + blk) * ROWS
        return node_id + (2 ** (level + 1) - 2), base

    def pick_sample(level, st, offset):
        row, base = table(level)

        def put(i, v):
            for c in range(4):
                st[8 * c + i // 16, pl.ds(offset + i % 16, 1), :] = v[:, 128 * c : 128 * c + 128]

        pick(level, base, row, lambda i: samp[level][pl.ds(i, 1), :], put)

    def pick_y(level, st, offset):
        row, base = table(level)

        def put(i, v):
            st[i // 8, pl.ds(offset + i % 8, 1), :] = v

        pick(level, base, row, lambda i: yref[pl.ds(i, 1), :], put)
        st[16:32, offset : offset + 8] = jnp.zeros((16, 8, 128), F32)

    def split_sample(l):
        hi, lo = split(samp[l][...])
        sh[l] = hi
        sl[l] = lo

    def split_probes(l):
        for i in range(7):
            t = prob[l, 128 * i : 128 * i + 128, :].T
            hi, lo = split(t)
            pth[l, :, 128 * i : 128 * i + 128] = hi
            ptl[l, :, 128 * i : 128 * i + 128] = lo

    def project(l, s):
        hi, lo = split(s)
        both = dot(sh[l], jnp.concatenate([hi, lo], axis=0), TRANSPOSED)
        return both[:, :SKEL] + both[:, SKEL:] + dot(sl[l], hi, TRANSPOSED)

    def test(l, yh, ycat):
        both = dot(pth[l], ycat)
        return both[:, :SKEL] + both[:, SKEL:] + dot(ptl[l], yh)

    def thin(a, b, dims=ROWMAJOR):
        ah, al = split(a)
        bh, bl = split(b)
        return dot(ah, bh, dims) + dot(ah, bl, dims) + dot(al, bh, dims)

    def couple(s, mt):
        m = mt.T
        spread = inverse(with_ridge(exact(m, m, TRANSPOSED), RIDGE))
        return exact(exact(s, mt), spread)

    def gram_inverse(s):
        return inverse(with_ridge(exact(s, s, TRANSPOSED), SAMPLES * RIDGE))

    loads.pop(0).wait()
    pick_sample(0, st_a0, 0)
    pl.semaphore_wait(barrier, len(ALL))
    share(st_a0, co_a0, A0)
    loads.pop(1).wait()
    scatter(st_a0, co_a0, rs_a0, A0, PLANE, in_plane)
    pick_sample(1, st_a1, 0)
    share(st_a1, co_a1, A1)
    split_sample(0)
    scatter(st_a1, co_a1, rs_a1, A1, PLANE, in_plane)
    arrive(A0 + 1)
    red_a0[...] = st_a0[gp] + jnp.sum(rs_a0[...], axis=0)
    exchange([(red_a0, ex_a0.at[i], m) for i, m in enumerate(HALF)], ex_a0, A0 + 2)
    loads.pop(3).wait()
    split_probes(0)
    arrive(A0 + 2)
    fu_a0[gp] = red_a0[...] + jnp.sum(ex_a0[...], axis=0)
    gather(fu_a0, A0 + 3, PLANE, gp)
    arrive(A1 + 1)
    red_a1[...] = st_a1[gp] + jnp.sum(rs_a1[...], axis=0)
    exchange([(red_a1, ex_a1, (0, 4))], ex_a1, A1 + 2)
    loads.pop(4).wait()
    split_probes(1)
    loads.pop(2).wait()
    pick_sample(2, st_d0, 24)
    forward(fu_a0, A0 + 3)
    arrive(A1 + 2)
    fu_a1[gp] = red_a1[...] + ex_a1[...]
    gather(fu_a1, A1 + 3, PLANE, gp)
    arrive(A0 + 4)

    s0 = blocks_to_matrix(fu_a0)
    y = project(0, s0)
    yref[...] = y
    yh, yl = split(y)
    ycat = jnp.concatenate([yh, yl], axis=1)
    st_b0[...] = test(0, yh, ycat).reshape(32, 16, 128)
    share(st_b0, co_b0, B0)
    st_c0[:, 0:16] = test(1, yh, ycat).reshape(32, 16, 128)
    pick_y(1, st_c0, 16)
    scatter(st_b0, co_b0, rs_b0, B0, PLANE, in_plane)
    share(st_c0, co_c0, C0)
    forward(fu_a1, A1 + 3)
    loads.pop(5).wait()
    split_probes(2)
    scatter(st_c0, co_c0, rs_c0, C0, PLANE, in_plane)
    g0 = gram_inverse(s0)
    arrive(B0 + 1)
    red_b0[...] = exact(st_b0[gp] + jnp.sum(rs_b0[...], axis=0), g0)
    exchange([(red_b0, ex_b0.at[i], m) for i, m in enumerate(ACROSS)], ex_b0, B0 + 2)
    arrive(C0 + 1)
    red_c0[...] = exact(st_c0[gp] + jnp.sum(rs_c0[...], axis=0), g0)
    exchange([(red_c0.at[pl.ds(0, 16)], ex_c0.at[i], m) for i, m in enumerate(ACROSS[2:])], ex_c0, C0 + 2)
    exchange([(red_c0.at[pl.ds(16, 8)], exy_c0, (0, 4))], exy_c0, C0 + 5)
    yh, yl = split(yref[...])
    st_d0[:, 0:16] = test(2, yh, jnp.concatenate([yh, yl], axis=1)).reshape(32, 16, 128)
    pick_y(2, st_d0, 16)
    share(st_d0, co_d0, D0)
    arrive(B0 + 2)
    fu_b0[gp] = jnp.sum(ex_b0[...], axis=0)
    gather(fu_b0, B0 + 3, PLANE, gp)
    arrive(C0 + 2)
    arrive(C0 + 5)
    fu_c0[gp, 0:16] = jnp.sum(ex_c0[...], axis=0)
    fu_c0[gp, 16:24] = red_c0[16:24] + exy_c0[...]
    gather(fu_c0, C0 + 3, PLANE, gp)
    basis[0] = thin(yref[...], g0)
    write(basis.at[0], basis_out.at[0], 0)
    split_sample(1)
    forward(fu_b0, B0 + 3)
    scatter(st_d0, co_d0, rs_d0, D0, NODE, in_node)
    arrive(B0 + 4)
    m0 = fu_b0[...].reshape(SAMPLES, SKEL)
    forward(fu_c0, C0 + 3)
    c0 = couple(s0, m0)
    coup[0] = c0

    arrive(A1 + 4)
    arrive(C0 + 4)
    k1t = exact(fu_c0[:, 0:16].reshape(SAMPLES, SKEL), c0, TRANSPOSED)
    s1 = blocks_to_matrix(fu_a1) - exact(fu_c0[0:16, 16:24].reshape(SKEL, SKEL), k1t, TRANSPOSED)
    y = project(1, s1) - thin(basis[0], exact(s1, k1t), TRANSPOSED)
    yref[...] = y
    yh, yl = split(y)
    ycat = jnp.concatenate([yh, yl], axis=1)
    st_b1[...] = test(1, yh, ycat).reshape(32, 16, 128)
    share(st_b1, co_b1, B1)
    st_d1[:, 0:16] = test(2, yh, ycat).reshape(32, 16, 128)
    pick_y(2, st_d1, 16)
    scatter(st_b1, co_b1, rs_b1, B1, PLANE, in_plane)
    share(st_d1, co_d1, D1)
    arrive(D0 + 1)
    sum_d0 = st_d0[gn] + jnp.sum(rs_d0[...], axis=0)
    red_d0[0:24] = exact(sum_d0[0:24], g0)
    red_d0[24:40] = sum_d0[24:40]
    exchange([(red_d0.at[pl.ds(0, 16)], ex_d0.at[i], m) for i, m in enumerate(((16, 0), (24, 0)))], ex_d0, D0 + 2)
    scatter(st_d1, co_d1, rs_d1, D1, NODE, in_node)
    g1 = gram_inverse(s1)
    arrive(B1 + 1)
    red_b1[...] = exact(st_b1[gp] + jnp.sum(rs_b1[...], axis=0), g1)
    exchange([(red_b1, ex_b1.at[i], m) for i, m in enumerate(((8, 0), (8, 4)))], ex_b1, B1 + 2)
    arrive(D1 + 1)
    red_d1[...] = exact(st_d1[gn] + jnp.sum(rs_d1[...], axis=0), g1)
    exchange([(red_d1.at[pl.ds(0, 16)], ex_d1, (12, 0))], ex_d1, D1 + 2)
    arrive(D0 + 2)
    swap_d0[...] = jnp.sum(ex_d0[...], axis=0)
    exchange([(swap_d0, exy_d0, (4, 0))], exy_d0, D0 + 5)
    arrive(B1 + 2)
    fu_b1[gp] = jnp.sum(ex_b1[...], axis=0)
    gather(fu_b1, B1 + 3, PLANE, gp)
    arrive(D0 + 5)
    fu_d0[gn, 0:16] = exy_d0[...]
    fu_d0[gn, 16:40] = red_d0[16:40]
    gather(fu_d0, D0 + 3, NODE, gn)
    arrive(D1 + 2)
    fu_d1[gn, 0:16] = ex_d1[...]
    fu_d1[gn, 16:24] = red_d1[16:24]
    gather(fu_d1, D1 + 3, NODE, gn)
    basis[1] = thin(yref[...], g1)
    write(basis.at[1], basis_out.at[1], 1)
    split_sample(2)
    forward(fu_b1, B1 + 3)
    arrive(B1 + 4)
    m1 = fu_b1[...].reshape(SAMPLES, SKEL)
    forward(fu_d0, D0 + 3)
    forward(fu_d1, D1 + 3)
    c1 = couple(s1, m1)
    coup[1] = c1

    arrive(D0 + 4)
    k2t = exact(fu_d0[:, 0:16].reshape(SAMPLES, SKEL), c0, TRANSPOSED)
    part2 = blocks_to_matrix(fu_d0[:, 24:40]) - exact(fu_d0[0:16, 16:24].reshape(SKEL, SKEL), k2t, TRANSPOSED)
    arrive(D1 + 4)
    k3t = exact(fu_d1[:, 0:16].reshape(SAMPLES, SKEL), c1, TRANSPOSED)
    s2 = part2 - exact(fu_d1[0:16, 16:24].reshape(SKEL, SKEL), k3t, TRANSPOSED)
    y = project(2, s2) - thin(basis[0], exact(s2, k2t), TRANSPOSED) - thin(basis[1], exact(s2, k3t), TRANSPOSED)
    yref[...] = y
    yh, yl = split(y)
    ycat = jnp.concatenate([yh, yl], axis=1)
    st_b2[...] = test(2, yh, ycat).reshape(32, 16, 128)
    share(st_b2, co_b2, B2)
    gram = with_ridge(exact(s2, s2, TRANSPOSED), SAMPLES * RIDGE)
    scatter(st_b2, co_b2, rs_b2, B2, SIBLING, in_node)
    red_b2[...] = inverse(gram)
    exchange([(red_b2, ex_b2, (4, 0))], ex_b2, B2 + 2)
    arrive(B2 + 1)
    fu_b2[gn] = jnp.sum(rs_b2[...], axis=0)
    gather(fu_b2, B2 + 3, NODE, gn)
    basis[2] = thin(yref[...], red_b2[...])
    write(basis.at[2], basis_out.at[2], 2)
    forward(fu_b2, B2 + 3)
    arrive(B2 + 2)
    arrive(B2 + 4)
    coup[2] = couple(s2, exact(fu_b2[...].reshape(SAMPLES, SKEL), ex_b2[...]))
    write(coup, coupling_out, 3)

    finish()


def vm(*shape, dtype=F32):
    return pltpu.VMEM(shape, dtype)


def local(sample, probes, skeleton_rows):
    def phase(rows, ex, received=15):
        return [
            vm(32, rows, 128), vm(16, rows, 128), vm(received, rows, 128), *ex, vm(32, rows, 128), vm(rows, 128),
        ]

    scratch = [
        vm(ROWS, SAMPLES), vm(ROWS, SAMPLES), vm(ROWS, SAMPLES), vm(3, ROWS, SAMPLES),
        vm(3, ROWS, SAMPLES, dtype=BF16), vm(3, ROWS, SAMPLES, dtype=BF16),
        vm(3, SAMPLES, ROWS, dtype=BF16), vm(3, SAMPLES, ROWS, dtype=BF16),
        vm(ROWS, SKEL), vm(3, ROWS, SKEL), vm(3, SKEL, SKEL),
        *phase(16, [vm(3, 16, 128)]),
        *phase(16, [vm(16, 128)]),
        *phase(16, [vm(4, 16, 128)]),
        *phase(24, [vm(2, 16, 128), vm(8, 128)]),
        *phase(40, [vm(2, 16, 128), vm(16, 128)]), vm(16, 128),
        *phase(16, [vm(2, 16, 128)]),
        *phase(24, [vm(16, 128)]),
        vm(32, 16, 128), vm(16, 16, 128), vm(16, 16, 128), vm(SKEL, SKEL), vm(32, 16, 128), vm(SKEL, SKEL),
        pltpu.SemaphoreType.DMA((48,)), pltpu.SemaphoreType.DMA((48,)),
        pltpu.SemaphoreType.DMA((6,)), pltpu.SemaphoreType.DMA((4,)),
    ]
    basis, coupling = pl.pallas_call(
        kernel,
        out_shape=(
            jax.ShapeDtypeStruct((3, ROWS, SKEL), F32),
            jax.ShapeDtypeStruct((3, SKEL, SKEL), F32),
        ),
        in_specs=[
            pl.BlockSpec(memory_space=pltpu.SMEM),
            pl.BlockSpec(memory_space=pl.ANY),
            pl.BlockSpec(memory_space=pl.ANY),
        ],
        out_specs=(pl.BlockSpec(memory_space=pl.ANY), pl.BlockSpec(memory_space=pl.ANY)),
        scratch_shapes=scratch,
        compiler_params=pltpu.CompilerParams(
            collective_id=0, has_side_effects=True, vmem_limit_bytes=52 * 2**20
        ),
    )(skeleton_rows, sample, probes)
    return basis, coupling[:, None]


def solution(mesh):
    placed = (P(None, ("leaf", "blk"), None), P(None, ("leaf", "blk"), None), P())
    return jax.shard_map(
        local,
        mesh=mesh,
        in_specs=placed,
        out_specs=(P(None, ("leaf", "blk"), None), P(None, "leaf", None, None)),
        check_vma=False,
    )
```

```python
import functools

import jax
import jax.numpy as jnp
from jax import lax
from jax.experimental import pallas as pl
from jax.experimental.pallas import tpu as pltpu
from jax.sharding import PartitionSpec as P

MESH = pl.DeviceIdType.MESH
F32 = jnp.float32
BF16 = jnp.bfloat16
ROWS = 896
SAMPLES = 512
SKEL = 128
RIDGE = 0.05
NROWS = 229376

STEP = 16
A0, A1, B0, C0, D0, B1, D1, B2 = range(0, 48, 6)

HOPS = (0, 1, 2, 1)
CORE = (1, 0)


def far(mask):
    a, b = mask
    return HOPS[a >> 1 & 3] + HOPS[b & 3] + (b >> 2)


def masks(leaf_masks, blk_masks):
    every = [(a, b) for a in leaf_masks for b in range(blk_masks)]
    return tuple(sorted((m for m in every if m != (0, 0)), key=lambda m: -far(m)))


NODE = masks((0, 2), 8)
PLANE = masks((0, 2, 4, 6), 4)
SIBLING = masks((4, 6), 8)
HALF = ((0, 4), (8, 0), (8, 4))
ACROSS = ((16, 0), (16, 4), (24, 0), (24, 4))
ALL = tuple(dict.fromkeys(ACROSS + ((12, 0),) + SIBLING + HALF + PLANE + NODE + (CORE,)))

ROWMAJOR = (((1,), (0,)), ((), ()))
TRANSPOSED = (((1,), (1,)), ((), ()))


def split(x):
    hi = x.astype(BF16)
    return hi, (x - hi.astype(F32)).astype(BF16)


def dot(a, b, dims=ROWMAJOR):
    return lax.dot_general(a, b, dims, preferred_element_type=F32)


def exact(a, b, dims=ROWMAJOR):
    return lax.dot_general(a, b, dims, precision=lax.Precision.HIGHEST, preferred_element_type=F32)


def inverse(a, halfway=None):
    lane = lax.broadcasted_iota(jnp.int32, (STEP, 128), 1)
    sub = lax.broadcasted_iota(jnp.int32, (STEP, 128), 0)
    lane_rest = lax.broadcasted_iota(jnp.int32, (128 - STEP, 128), 1)

    def body(_, a):
        p = a[0:STEP]
        c = [jnp.broadcast_to(p[:, i : i + 1], (STEP, 128)) for i in range(STEP)]
        for i in range(STEP):
            d = 1.0 / jnp.broadcast_to(c[i][i : i + 1], (STEP, 128))
            m = jnp.where(sub == i, 1.0 - d, c[i] * d)
            row = jnp.where(lane == i, 1.0, jnp.broadcast_to(p[i : i + 1], (STEP, 128)))
            z = jnp.where(lane == i, jnp.where(sub == i, 1.0, 0.0), p)
            p = z - m * row
            for j in range(i + 1, STEP):
                c[j] = c[j] - m * jnp.broadcast_to(c[j][i : i + 1], (STEP, 128))
        r = a[STEP:]
        n = jnp.where(lane_rest < STEP, 0.0, r)
        for i in range(STEP):
            n = n - r[:, i : i + 1] * p[i : i + 1]
        return pltpu.roll(jnp.concatenate([n, p], 0), 128 - STEP, 1)

    a = lax.fori_loop(0, 64 // STEP, body, a)
    if halfway:
        halfway()
    return lax.fori_loop(0, 64 // STEP, body, a)


def with_ridge(a, ridge):
    i = lax.broadcasted_iota(jnp.int32, (SKEL, SKEL), 0)
    j = lax.broadcasted_iota(jnp.int32, (SKEL, SKEL), 1)
    return a + jnp.where(i == j, ridge, 0.0)


def blocks_to_matrix(full):
    return jnp.concatenate([full[8 * c : 8 * c + 8].reshape(SKEL, 128) for c in range(4)], axis=1)


def kernel(
    rows_ref, sample_ref, probes_ref, basis_out, coupling_out,
    samp0, samp1, samp2, prob, sh, sl, pth, ptl, yref, basis, coup,
    st_a0, co_a0, rs_a0, ex_a0, fu_a0, red_a0,
    st_a1, co_a1, rs_a1, ex_a1, fu_a1, red_a1,
    st_b0, co_b0, rs_b0, ex_b0, fu_b0, red_b0,
    st_c0, co_c0, rs_c0, ex_c0, exy_c0, fu_c0, red_c0,
    st_d0, co_d0, rs_d0, ex_d0, exy_d0, fu_d0, red_d0, swap_d0,
    st_b1, co_b1, rs_b1, ex_b1, fu_b1, red_b1,
    st_d1, co_d1, rs_d1, ex_d1, fu_d1, red_d1,
    st_b2, co_b2, rs_b2, ex_b2, fu_b2, red_b2,
    ssem, rsem, insem, outsem,
):
    samp = (samp0, samp1, samp2)
    leaf = lax.axis_index("leaf")
    blk = lax.axis_index("blk")
    leaf_step = [(1 - 2 * ((leaf // (1 << k)) % 2)) * (1 << k) for k in range(5)]
    blk_step = [(1 - 2 * ((blk // (1 << k)) % 2)) * (1 << k) for k in range(3)]

    def at(mask):
        a, b = leaf, blk
        for k in range(5):
            if mask[0] >> k & 1:
                a = a + leaf_step[k]
        for k in range(3):
            if mask[1] >> k & 1:
                b = b + blk_step[k]
        return a, b

    core = leaf % 2
    own = pl.ds(16 * core, 16)
    other = pl.ds(16 * (1 - core), 16)

    def in_node(a, b):
        return (a % 2) * 16 + (a // 2 % 2) * 8 + b

    def in_plane(a, b):
        return (a % 2) * 16 + (a // 2 % 4) * 4 + b % 4

    gn = in_node(leaf, blk)
    gp = in_plane(leaf, blk)

    loads = {}
    for l in range(3):
        loads[l] = pltpu.make_async_copy(sample_ref.at[l], samp[l], insem.at[l])
    for l in range(3):
        loads[3 + l] = pltpu.make_async_copy(probes_ref.at[l], prob.at[l], insem.at[3 + l])
    for c in loads.values():
        c.start()

    barrier = pltpu.get_barrier_semaphore()
    for m in ALL:
        pl.semaphore_signal(barrier, inc=1, device_id=at(m), device_id_type=MESH)

    leaving, landing, writing = [], {}, []

    def wait_bytes(ref, sem):
        pltpu.make_async_copy(ref, ref, sem).wait()

    def start(ref, stage):
        leaving.append((ref, stage))
        landing[stage] = ref

    def arrive(stage):
        wait_bytes(landing.pop(stage), rsem.at[stage])

    def write(src, dst, i):
        copy = pltpu.make_async_copy(src, dst, outsem.at[i])
        copy.start()
        writing.append(copy)

    def finish():
        for copy in loads.values():
            copy.wait()
        for stage in tuple(landing):
            arrive(stage)
        for ref, stage in leaving:
            wait_bytes(ref, ssem.at[stage])
        for copy in writing:
            copy.wait()

    def send(src, dst, stage, to):
        pltpu.make_async_remote_copy(
            src_ref=src, dst_ref=dst, send_sem=ssem.at[stage], recv_sem=rsem.at[stage],
            device_id=to, device_id_type=MESH,
        ).start()

    def share(st, co, stage):
        send(st.at[other], co, stage, at(CORE))
        start(co, stage)

    def scatter(st, co, rs, stage, group, number):
        arrive(stage)
        st[own] = st[own] + co[...]
        for i, m in enumerate(group):
            to = at(m)
            send(st.at[number(*to)], rs.at[i], stage + 1, to)
        start(rs, stage + 1)

    def exchange(pieces, ex, stage):
        for src, dst, m in pieces:
            send(src, dst, stage, at(m))
        start(ex, stage)

    def gather(fu, stage, group, mine):
        for m in group:
            send(fu.at[mine], fu.at[mine], stage, at(m))
        start(fu.at[pl.ds(0, 15)], stage)

    def forward(fu, stage):
        arrive(stage)
        send(fu.at[own], fu.at[own], stage + 1, at(CORE))
        start(fu.at[other], stage + 1)

    def pick(level, base, table_row, source, put):
        def one(i, _):
            place = rows_ref[table_row, i] + base
            here = (place >= 0) & (place < ROWS)
            safe = jnp.clip(place, 0, ROWS - 1)
            put(i, jnp.where(here, source(safe), 0.0))
            return 0

        lax.fori_loop(0, SKEL, one, 0, unroll=8)

    def table(level):
        node_id = leaf // (1 << (4 - level))
        base = node_id * (NROWS >> (level + 1)) - (leaf * 8 + blk) * ROWS
        return node_id + (2 ** (level + 1) - 2), base

    def pick_sample(level, st, offset):
        row, base = table(level)

        def put(i, v):
            for c in range(4):
                st[8 * c + i // 16, pl.ds(offset + i % 16, 1), :] = v[:, 128 * c : 128 * c + 128]

        pick(level, base, row, lambda i: samp[level][pl.ds(i, 1), :], put)

    def pick_y(level, st, offset):
        row, base = table(level)

        def put(i, v):
            st[i // 8, pl.ds(offset + i % 8, 1), :] = v

        pick(level, base, row, lambda i: yref[pl.ds(i, 1), :], put)
        st[16:32, offset : offset + 8] = jnp.zeros((16, 8, 128), F32)

    def split_sample(l):
        hi, lo = split(samp[l][...])
        sh[l] = hi
        sl[l] = lo

    def split_probes(l):
        for i in range(7):
            t = prob[l, 128 * i : 128 * i + 128, :].T
            hi, lo = split(t)
            pth[l, :, 128 * i : 128 * i + 128] = hi
            ptl[l, :, 128 * i : 128 * i + 128] = lo

    def project(l, s):
        hi, lo = split(s)
        both = dot(sh[l], jnp.concatenate([hi, lo], axis=0), TRANSPOSED)
        return both[:, :SKEL] + both[:, SKEL:] + dot(sl[l], hi, TRANSPOSED)

    def test(l, yh, ycat):
        both = dot(pth[l], ycat)
        return both[:, :SKEL] + both[:, SKEL:] + dot(ptl[l], yh)

    def thin(a, b, dims=ROWMAJOR):
        ah, al = split(a)
        bh, bl = split(b)
        return dot(ah, bh, dims) + dot(ah, bl, dims) + dot(al, bh, dims)

    def couple(s, mt, halfway=None):
        m = mt.T
        spread = inverse(with_ridge(exact(m, m, TRANSPOSED), RIDGE), halfway)
        return exact(exact(s, mt), spread)

    def gram_inverse(s, halfway=None):
        return inverse(with_ridge(exact(s, s, TRANSPOSED), SAMPLES * RIDGE), halfway)

    loads.pop(0).wait()
    pick_sample(0, st_a0, 0)
    pl.semaphore_wait(barrier, len(ALL))
    share(st_a0, co_a0, A0)
    loads.pop(1).wait()
    scatter(st_a0, co_a0, rs_a0, A0, PLANE, in_plane)
    pick_sample(1, st_a1, 0)
    share(st_a1, co_a1, A1)
    split_sample(0)
    scatter(st_a1, co_a1, rs_a1, A1, PLANE, in_plane)
    arrive(A0 + 1)
    red_a0[...] = st_a0[gp] + jnp.sum(rs_a0[...], axis=0)
    exchange([(red_a0, ex_a0.at[i], m) for i, m in enumerate(HALF)], ex_a0, A0 + 2)
    loads.pop(3).wait()
    split_probes(0)
    arrive(A0 + 2)
    fu_a0[gp] = red_a0[...] + jnp.sum(ex_a0[...], axis=0)
    gather(fu_a0, A0 + 3, PLANE, gp)
    arrive(A1 + 1)
    red_a1[...] = st_a1[gp] + jnp.sum(rs_a1[...], axis=0)
    exchange([(red_a1, ex_a1, (0, 4))], ex_a1, A1 + 2)
    loads.pop(4).wait()
    split_probes(1)
    loads.pop(2).wait()
    pick_sample(2, st_d0, 24)
    loads.pop(5).wait()
    split_probes(2)
    forward(fu_a0, A0 + 3)
    arrive(A1 + 2)
    fu_a1[gp] = red_a1[...] + ex_a1[...]
    gather(fu_a1, A1 + 3, PLANE, gp)
    arrive(A0 + 4)

    s0 = blocks_to_matrix(fu_a0)
    y = project(0, s0)
    yref[...] = y
    yh, yl = split(y)
    ycat = jnp.concatenate([yh, yl], axis=1)
    st_b0[...] = test(0, yh, ycat).reshape(32, 16, 128)
    share(st_b0, co_b0, B0)
    st_c0[:, 0:16] = test(1, yh, ycat).reshape(32, 16, 128)
    pick_y(1, st_c0, 16)
    scatter(st_b0, co_b0, rs_b0, B0, PLANE, in_plane)
    share(st_c0, co_c0, C0)
    scatter(st_c0, co_c0, rs_c0, C0, PLANE, in_plane)
    g0 = gram_inverse(s0, lambda: forward(fu_a1, A1 + 3))
    arrive(B0 + 1)
    red_b0[...] = exact(st_b0[gp] + jnp.sum(rs_b0[...], axis=0), g0)
    exchange([(red_b0, ex_b0.at[i], m) for i, m in enumerate(ACROSS)], ex_b0, B0 + 2)
    arrive(C0 + 1)
    red_c0[...] = exact(st_c0[gp] + jnp.sum(rs_c0[...], axis=0), g0)
    exchange([(red_c0.at[pl.ds(0, 16)], ex_c0.at[i], m) for i, m in enumerate(ACROSS[2:])], ex_c0, C0 + 2)
    exchange([(red_c0.at[pl.ds(16, 8)], exy_c0, (0, 4))], exy_c0, C0 + 5)
    yh, yl = split(yref[...])
    st_d0[:, 0:16] = test(2, yh, jnp.concatenate([yh, yl], axis=1)).reshape(32, 16, 128)
    pick_y(2, st_d0, 16)
    share(st_d0, co_d0, D0)
    arrive(B0 + 2)
    fu_b0[gp] = jnp.sum(ex_b0[...], axis=0)
    gather(fu_b0, B0 + 3, PLANE, gp)
    arrive(C0 + 2)
    arrive(C0 + 5)
    fu_c0[gp, 0:16] = jnp.sum(ex_c0[...], axis=0)
    fu_c0[gp, 16:24] = red_c0[16:24] + exy_c0[...]
    gather(fu_c0, C0 + 3, PLANE, gp)
    basis[0] = thin(yref[...], g0)
    write(basis.at[0], basis_out.at[0], 0)
    split_sample(1)
    forward(fu_b0, B0 + 3)
    scatter(st_d0, co_d0, rs_d0, D0, NODE, in_node)
    arrive(B0 + 4)
    m0 = fu_b0[...].reshape(SAMPLES, SKEL)
    c0 = couple(s0, m0, lambda: forward(fu_c0, C0 + 3))
    coup[0] = c0

    arrive(A1 + 4)
    arrive(C0 + 4)
    k1t = exact(fu_c0[:, 0:16].reshape(SAMPLES, SKEL), c0, TRANSPOSED)
    s1 = blocks_to_matrix(fu_a1) - exact(fu_c0[0:16, 16:24].reshape(SKEL, SKEL), k1t, TRANSPOSED)
    y = project(1, s1) - thin(basis[0], exact(s1, k1t), TRANSPOSED)
    yref[...] = y
    yh, yl = split(y)
    ycat = jnp.concatenate([yh, yl], axis=1)
    st_b1[...] = test(1, yh, ycat).reshape(32, 16, 128)
    share(st_b1, co_b1, B1)
    st_d1[:, 0:16] = test(2, yh, ycat).reshape(32, 16, 128)
    pick_y(2, st_d1, 16)
    scatter(st_b1, co_b1, rs_b1, B1, PLANE, in_plane)
    share(st_d1, co_d1, D1)
    arrive(D0 + 1)
    sum_d0 = st_d0[gn] + jnp.sum(rs_d0[...], axis=0)
    red_d0[0:24] = exact(sum_d0[0:24], g0)
    red_d0[24:40] = sum_d0[24:40]
    exchange([(red_d0.at[pl.ds(0, 16)], ex_d0.at[i], m) for i, m in enumerate(((16, 0), (24, 0)))], ex_d0, D0 + 2)
    scatter(st_d1, co_d1, rs_d1, D1, NODE, in_node)

    def swap():
        arrive(D0 + 2)
        swap_d0[...] = jnp.sum(ex_d0[...], axis=0)
        exchange([(swap_d0, exy_d0, (4, 0))], exy_d0, D0 + 5)

    g1 = gram_inverse(s1, swap)
    arrive(B1 + 1)
    red_b1[...] = exact(st_b1[gp] + jnp.sum(rs_b1[...], axis=0), g1)
    exchange([(red_b1, ex_b1.at[i], m) for i, m in enumerate(((8, 0), (8, 4)))], ex_b1, B1 + 2)
    arrive(D0 + 5)
    fu_d0[gn, 0:16] = exy_d0[...]
    fu_d0[gn, 16:40] = red_d0[16:40]
    gather(fu_d0, D0 + 3, NODE, gn)
    arrive(D1 + 1)
    red_d1[...] = exact(st_d1[gn] + jnp.sum(rs_d1[...], axis=0), g1)
    exchange([(red_d1.at[pl.ds(0, 16)], ex_d1, (12, 0))], ex_d1, D1 + 2)
    arrive(B1 + 2)
    fu_b1[gp] = jnp.sum(ex_b1[...], axis=0)
    gather(fu_b1, B1 + 3, PLANE, gp)
    arrive(D1 + 2)
    fu_d1[gn, 0:16] = ex_d1[...]
    fu_d1[gn, 16:24] = red_d1[16:24]
    gather(fu_d1, D1 + 3, NODE, gn)
    basis[1] = thin(yref[...], g1)
    write(basis.at[1], basis_out.at[1], 1)
    split_sample(2)
    forward(fu_b1, B1 + 3)
    arrive(B1 + 4)
    m1 = fu_b1[...].reshape(SAMPLES, SKEL)
    forward(fu_d0, D0 + 3)
    c1 = couple(s1, m1, lambda: forward(fu_d1, D1 + 3))
    coup[1] = c1

    arrive(D0 + 4)
    k2t = exact(fu_d0[:, 0:16].reshape(SAMPLES, SKEL), c0, TRANSPOSED)
    part2 = blocks_to_matrix(fu_d0[:, 24:40]) - exact(fu_d0[0:16, 16:24].reshape(SKEL, SKEL), k2t, TRANSPOSED)
    arrive(D1 + 4)
    k3t = exact(fu_d1[:, 0:16].reshape(SAMPLES, SKEL), c1, TRANSPOSED)
    s2 = part2 - exact(fu_d1[0:16, 16:24].reshape(SKEL, SKEL), k3t, TRANSPOSED)
    y = project(2, s2) - thin(basis[0], exact(s2, k2t), TRANSPOSED) - thin(basis[1], exact(s2, k3t), TRANSPOSED)
    yref[...] = y
    yh, yl = split(y)
    ycat = jnp.concatenate([yh, yl], axis=1)
    st_b2[...] = test(2, yh, ycat).reshape(32, 16, 128)
    share(st_b2, co_b2, B2)
    gram = with_ridge(exact(s2, s2, TRANSPOSED), SAMPLES * RIDGE)
    scatter(st_b2, co_b2, rs_b2, B2, SIBLING, in_node)
    red_b2[...] = inverse(gram)
    exchange([(red_b2, ex_b2, (4, 0))], ex_b2, B2 + 2)
    arrive(B2 + 1)
    fu_b2[gn] = jnp.sum(rs_b2[...], axis=0)
    gather(fu_b2, B2 + 3, NODE, gn)
    basis[2] = thin(yref[...], red_b2[...])
    write(basis.at[2], basis_out.at[2], 2)
    forward(fu_b2, B2 + 3)
    arrive(B2 + 2)
    arrive(B2 + 4)
    coup[2] = couple(s2, exact(fu_b2[...].reshape(SAMPLES, SKEL), ex_b2[...]))
    write(coup, coupling_out, 3)

    finish()


def vm(*shape, dtype=F32):
    return pltpu.VMEM(shape, dtype)


def local(sample, probes, skeleton_rows):
    def phase(rows, ex, received=15):
        return [
            vm(32, rows, 128), vm(16, rows, 128), vm(received, rows, 128), *ex, vm(32, rows, 128), vm(rows, 128),
        ]

    scratch = [
        vm(ROWS, SAMPLES), vm(ROWS, SAMPLES), vm(ROWS, SAMPLES), vm(3, ROWS, SAMPLES),
        vm(3, ROWS, SAMPLES, dtype=BF16), vm(3, ROWS, SAMPLES, dtype=BF16),
        vm(3, SAMPLES, ROWS, dtype=BF16), vm(3, SAMPLES, ROWS, dtype=BF16),
        vm(ROWS, SKEL), vm(3, ROWS, SKEL), vm(3, SKEL, SKEL),
        *phase(16, [vm(3, 16, 128)]),
        *phase(16, [vm(16, 128)]),
        *phase(16, [vm(4, 16, 128)]),
        *phase(24, [vm(2, 16, 128), vm(8, 128)]),
        *phase(40, [vm(2, 16, 128), vm(16, 128)]), vm(16, 128),
        *phase(16, [vm(2, 16, 128)]),
        *phase(24, [vm(16, 128)]),
        vm(32, 16, 128), vm(16, 16, 128), vm(16, 16, 128), vm(SKEL, SKEL), vm(32, 16, 128), vm(SKEL, SKEL),
        pltpu.SemaphoreType.DMA((48,)), pltpu.SemaphoreType.DMA((48,)),
        pltpu.SemaphoreType.DMA((6,)), pltpu.SemaphoreType.DMA((4,)),
    ]
    basis, coupling = pl.pallas_call(
        kernel,
        out_shape=(
            jax.ShapeDtypeStruct((3, ROWS, SKEL), F32),
            jax.ShapeDtypeStruct((3, SKEL, SKEL), F32),
        ),
        in_specs=[
            pl.BlockSpec(memory_space=pltpu.SMEM),
            pl.BlockSpec(memory_space=pl.ANY),
            pl.BlockSpec(memory_space=pl.ANY),
        ],
        out_specs=(pl.BlockSpec(memory_space=pl.ANY), pl.BlockSpec(memory_space=pl.ANY)),
        scratch_shapes=scratch,
        compiler_params=pltpu.CompilerParams(
            collective_id=0, has_side_effects=True, vmem_limit_bytes=52 * 2**20
        ),
    )(skeleton_rows, sample, probes)
    return basis, coupling[:, None]


def solution(mesh):
    placed = (P(None, ("leaf", "blk"), None), P(None, ("leaf", "blk"), None), P())
    return jax.shard_map(
        local,
        mesh=mesh,
        in_specs=placed,
        out_specs=(P(None, ("leaf", "blk"), None), P(None, "leaf", None, None)),
        check_vma=False,
    )
```
